1024 devices in a mesh: rep: 32 (over y, x_hi), exp: 32 (over x_lo, z, core).
Axes of the slice: x: 8 (x_hi: 4, x_lo: 2; x = x_hi * 2 + x_lo), y: 8, z: 8, core: 2. Of those that a mesh axis runs over, the one named last changes fastest.
Arguments:
- cotangent: bfloat16 [131072, 4096], P(('rep', 'exp')), may hold values from -2.5 to 2.5
- routes: int32 [131072, 1], P(('rep', 'exp')), may hold values from 0 to 31; in each aligned block of 128 rows (0 to 127, 128 to 255, ...) at most 6 rows name the same one
- gate_weight: float32 [131072, 1], P(('rep', 'exp')), may hold values from 0.1 to 1
- down_weight: bfloat16 [32, 4096, 768], P('exp'), may hold values from -0.21875 to 0.21875
- saved_pre: bfloat16 [32, 32, 192, 1536], P('rep', 'exp'), may hold values from -6 to 6
Outputs:
- weight_grad: float32 [32, 4096, 768], P('exp', 'rep')
- input_grads: bfloat16 [32, 32, 192, 1536], P('rep', 'exp')
- token_grad: float32 [131072, 1], P(('rep', 'exp'))
The draws below stay inside these ranges and needn't reach their ends.
Inputs may be any that keep to these rules, and one draw needn't show every extreme that they name: `routes`: the rows of one device name each expert at most 6 times; in every draw some device names some expert exactly 6 times.
All inputs are finite; a program needn't handle non-finite values.
Results may differ from the reference program's by a relative error of at most 0.019.
Values may be sent and summed in bfloat16 or wider, within the bound.
A program may use at most 64 MiB of HBM per device.

```python
import math
import jax
import jax.numpy as jnp
import numpy as np
from jax import lax

D = 4096
FF = 768
TOK_DEV = 128
EXPERTS = 32
CAP = 6
ROWS = 192
TOKENS = 131072
N_REP = 32
N_EXP = 32


def strengthened(values, stream_key, source, target, shards_of, factor):
    def block_of(dim):
        return (jnp.arange(values.shape[dim]) // (values.shape[dim] // shards_of)).reshape((-1,) + (1,) * (values.ndim - 1 - dim))

    one_side = jax.random.permutation(stream_key, shards_of)[block_of(target)]
    second = (block_of(target) + shards_of // 2) % shards_of
    return jnp.where((block_of(source) == one_side) | (block_of(source) == second), factor * values, values)


def block_scale(key, shape, cuts, least, largest):
    gain = 1.0
    for dim, shards_of in cuts:
        draws = jax.random.uniform(jax.random.fold_in(jax.random.fold_in(key, 6), dim), (shards_of,), jnp.float32, least / len(cuts), largest / len(cuts))
        gain = gain * jnp.repeat(jnp.exp(draws), shape[dim] // shards_of).reshape((-1,) + (1,) * (len(shape) - 1 - dim))
    return gain


def routed_block(stream_key, own, number, rows, amount, top, bound, lean):
    ranking = jax.random.permutation(stream_key, amount)
    heavy_load, common = portions_of(amount, rows * top, bound, lean, True), portions_of(amount, rows * top, bound, lean, False)
    places = jnp.arange(amount)

    def named(sizes, rotation):
        used = int((sizes > 0).sum())
        fixed = max(1, used // 4)
        passed = fixed + (places - fixed + rotation * (used - fixed)) % max(1, amount - fixed)
        return jnp.zeros((amount,), jnp.int32).at[ranking[jnp.where(places < fixed, places, passed)]].set(jnp.asarray(sizes, jnp.int32))

    sizes = jnp.where(number % 4 == 0, named(heavy_load, number // 4), named(common, number - number // 4 - 1))
    mixed = jax.random.permutation(jax.random.fold_in(own, 3), amount)
    giver, receiver = mixed[0:amount // 2 * 2:2], mixed[1:amount // 2 * 2:2]
    room = jnp.minimum(sizes[giver] - 1, bound - sizes[receiver]) // 2
    room = jnp.where((giver == ranking[0]) | (receiver == ranking[0]) | (sizes[receiver] == 0), 0, jnp.maximum(room, 0))
    passed = jax.random.randint(jax.random.fold_in(own, 4), (amount // 2,), 0, 1 << 20) % (room + 1)
    sizes = sizes.at[giver].add(-passed).at[receiver].add(passed)
    items = jnp.searchsorted(jnp.cumsum(sizes), jnp.arange(rows * top), side="right").astype(jnp.int32)
    grid = items.reshape(top, rows).T
    grid = grid[jax.random.permutation(jax.random.fold_in(own, 1), rows)]
    rotation = jax.random.randint(jax.random.fold_in(own, 2), (rows, 1), 0, top)
    return jnp.take_along_axis(grid, (jnp.arange(top)[None, :] + rotation) % top, axis=1)


def portions_of(count, total, bound, slope, full):
    portions = [(1 << 20) // math.isqrt(grade ** slope) + 1 for grade in range(1, count + 1)]
    largest = bound if full else min(bound, max(-(-total // count), total * portions[0] // sum(portions)))
    least = 1 if total - largest >= count - 1 else 0
    given, spare = [largest] + [least] * (count - 1), total - largest - least * (count - 1)
    while spare > 0:
        movable = [i for i in range(1, count) if given[i] < largest] or [i for i in range(1, count) if given[i] < bound]
        mass, remaining = sum([portions[i] for i in movable]), spare
        for i in movable:
            addition = min(bound - given[i], max(1, remaining * portions[i] // mass), spare)
            given[i] = given[i] + addition
            spare = spare - addition
    return np.array(given)


def centred(rng, shape, width, limit, cuts=(), held_as=jnp.bfloat16):
    values = jax.random.normal(rng, shape, jnp.float32) * width
    if len(cuts) > 0:
        values = block_scale(rng, shape, cuts, -0.22, 0.18) * values
    return jnp.clip(values, min=-limit, max=limit).astype(held_as)


def bell_draw_with(rng, shape, scale, reach, split, heavy, held_as=jnp.bfloat16):
    entries = scale * jax.random.normal(rng, shape, jnp.float32)
    if split:
        entries = entries * block_scale(rng, shape, split, -0.22, 0.18)
    return jnp.clip(strengthened(entries, jax.random.fold_in(rng, 3), *heavy), -reach, reach).astype(held_as)


def setup_inputs(seed: int = 0) -> dict:
    keys = jax.random.split(jax.random.key(seed), 6)
    cotangent = bell_draw_with(keys[0], (TOKENS, D), 0.1, 2.5, ((0, 1024),), (0, 1, 1024, 6.0))
    routes_keys = jax.random.split(jax.random.fold_in(keys[1], 1), TOKENS // TOK_DEV)
    routes_turns = jax.random.permutation(jax.random.fold_in(keys[1], 3), TOKENS // TOK_DEV)
    routes = jax.vmap(lambda own, number: routed_block(jax.random.fold_in(keys[1], 2), own, number, TOK_DEV, EXPERTS, 1, CAP, 2))(routes_keys, routes_turns).reshape((TOKENS, 1))
    gate_weight = jnp.clip(jnp.exp(math.log(1.0) - 2.3025851 * jax.random.uniform(keys[2], (TOKENS, 1), jnp.float32) ** block_scale(keys[2], (TOKENS, 1), ((0, 1024),), -0.2, 0.2)), 0.1, 1.0)
    down_weight = centred(keys[3], (EXPERTS, D, FF), FF ** -0.5, 0.21875, ((0, 32),))
    saved_pre = centred(keys[4], (N_REP, EXPERTS, ROWS, 2 * FF), 1.0, 6.0, ((0, 32), (1, 32)))
    return {"cotangent": cotangent, "routes": routes, "gate_weight": gate_weight, "down_weight": down_weight, "saved_pre": saved_pre}


def slot_table(expert_ids):
    experts = jnp.arange(EXPERTS, dtype=jnp.int32)
    one_hot = (expert_ids[:, :, None] == experts[None, None, :]).astype(jnp.int32)
    earlier = jnp.cumsum(one_hot, axis=1) - one_hot
    position = jnp.sum(earlier * one_hot, axis=2)
    source = jnp.arange(N_EXP, dtype=jnp.int32)[:, None]
    return (source * CAP + position).astype(jnp.int32)


def reference(cotangent, routes, gate_weight, down_weight, saved_pre):
    wide_weight = down_weight.astype(jnp.float32)
    block_rows = N_EXP * TOK_DEV

    def replica(running, replica_index):
        begin_row = replica_index * block_rows
        cot_rows = lax.dynamic_slice_in_dim(cotangent, begin_row, block_rows, 0)
        expert_ids = lax.dynamic_slice_in_dim(routes, begin_row, block_rows, 0)[:, 0].reshape(N_EXP, TOK_DEV)
        weights = lax.dynamic_slice_in_dim(gate_weight, begin_row, block_rows, 0)[:, 0].reshape(N_EXP, TOK_DEV).astype(jnp.bfloat16)
        slot_rows = slot_table(expert_ids)
        arrived = jnp.zeros((EXPERTS, ROWS, D), jnp.bfloat16).at[expert_ids, slot_rows].set(cot_rows.reshape(N_EXP, TOK_DEV, D))
        weight_sent = jnp.zeros((EXPERTS, ROWS), jnp.bfloat16).at[expert_ids, slot_rows].set(weights)
        saved_pair = lax.dynamic_index_in_dim(saved_pre, replica_index, 0, keepdims=False).astype(jnp.float32)
        gate_pre = saved_pair[..., :FF]
        up_pre = saved_pair[..., FF:]
        arrived_wide = arrived.astype(jnp.float32)
        pulled = jnp.einsum('esd,edf->esf', arrived_wide, wide_weight)
        sigmoid_gate = jax.nn.sigmoid(gate_pre)
        silu_gate = gate_pre * sigmoid_gate
        hidden = silu_gate * up_pre
        router = jnp.sum(pulled * hidden, axis=2)
        scale_col = weight_sent.astype(jnp.float32)[..., None]
        hidden_grad = scale_col * pulled
        gate_grad = hidden_grad * up_pre * sigmoid_gate * (1.0 + gate_pre * (1.0 - sigmoid_gate))
        up_grad = hidden_grad * silu_gate
        pair_grads = jnp.concatenate([gate_grad, up_grad], axis=2).astype(jnp.bfloat16)
        scaled = (scale_col * hidden).astype(jnp.bfloat16)
        partial_value = jnp.einsum('esd,esf->edf', arrived_wide, scaled.astype(jnp.float32)).astype(jnp.bfloat16)
        running = running + partial_value.astype(jnp.float32)
        token_part = router[expert_ids, slot_rows].reshape(block_rows, 1)
        return running, (pair_grads, token_part)

    start_sum = jnp.zeros((EXPERTS, D, FF), jnp.float32)
    weight_grad, (input_grads, token_parts) = lax.scan(replica, start_sum, jnp.arange(N_REP, dtype=jnp.int32))
    return weight_grad, input_grads, token_parts.reshape(TOKENS, 1)
```

```python
import functools

import jax
import jax.numpy as jnp
from jax import lax
from jax.experimental import pallas as pl
from jax.experimental.pallas import tpu as pltpu
from jax.sharding import PartitionSpec as P

MESH = pl.DeviceIdType.MESH
BF = jnp.bfloat16
F32 = jnp.float32
CAP = 6
GROUP = 8
SUBS = 2


def dot(a, b, lhs=1, **kw):
    return lax.dot_general(a, b, (((lhs,), (0,)), ((), ())), preferred_element_type=F32, **kw)


def iota(shape, dim):
    return lax.broadcasted_iota(jnp.int32, shape, dim).astype(F32)


def kernel(
    ny, nx, peers,
    cot, routes, gate, weight_hbm, saved,
    grad_out, pair_out, token_out,
    weight, send, recv, arrived, place6, place8, swap, select,
    gate_send, gate_recv, router_send, router_recv,
    hidden, scale, scaled, pulled, ring_send, ring_recv, chunk, x_send, x_recv,
    weight_sem, send_sem, recv_sem, gate_ssem, gate_rsem, router_ssem, router_rsem,
    ring_ssem, ring_rsem, x_ssem, x_rsem,
):
    tokens = cot.shape[0]
    slots = peers * CAP
    groups = peers // GROUP
    width = weight.shape[1]
    half = cot.shape[1] // ny // 2
    steps = ny // 2
    rows = GROUP * CAP
    block = GROUP * rows
    msg = GROUP * CAP
    lanes = half // 2
    sub_w = width // SUBS
    out_rows = 2 * half // nx
    rep, me = lax.axis_index("rep"), lax.axis_index("exp")
    y, xh = rep // nx, rep % nx
    right = ((y + 1) % ny) * nx + xh
    left = ((y + ny - 1) % ny) * nx + xh

    weight_copy = pltpu.make_async_copy(weight_hbm, weight, weight_sem)
    weight_copy.start()

    barrier = pltpu.get_barrier_semaphore()

    @pl.loop(1, peers)
    def _(i):
        pl.semaphore_signal(
            barrier, inc=1, device_id=(rep, (me + i) % peers), device_id_type=MESH
        )

    for other in (left, right):
        pl.semaphore_signal(barrier, inc=1, device_id=(other, me), device_id_type=MESH)
    for i in range(1, nx):
        pl.semaphore_signal(
            barrier, inc=1, device_id=(y * nx + (xh + i) % nx, me), device_id_type=MESH
        )

    def column(which, k):
        at = (y + ny - 1 - k) % ny if which == 0 else (y + 1 + k) % ny
        return pl.multiple_of((at * 2 + which) * half, half)

    ids = routes[...].astype(F32)
    one_hot = ids == iota((tokens, peers), 1)
    below = (iota((tokens, tokens), 0) > iota((tokens, tokens), 1)).astype(F32).astype(BF)
    earlier = dot(below, one_hot.astype(F32).astype(BF))
    position = jnp.sum(jnp.where(one_hot, earlier, 0.0), axis=1, keepdims=True)
    place6[...] = (ids * CAP + position == iota((tokens, slots), 1)).astype(F32).astype(BF)
    place8[...] = (ids * 8 + position == iota((tokens, peers * 8), 1)).astype(F32)
    gate_b = jnp.broadcast_to(gate[...].astype(BF), (tokens, 128))
    gate_send[...] = dot(place8[...].astype(BF), gate_b, 0)

    r = iota((block, 1), 0)
    a = jnp.floor((r + 0.5) * (1.0 / rows))
    ab = jnp.floor((r + 0.5) * (1.0 / CAP))
    source = (ab - GROUP * a) * rows + a * CAP + (r - CAP * ab)
    swap[...] = (source == iota((block, block), 1)).astype(F32).astype(BF)
    r = iota((slots, 1), 0)
    spread = r + (8 - CAP) * jnp.floor((r + 0.5) * (1.0 / CAP))
    select[...] = (spread == iota((slots, peers * 8), 1)).astype(F32)

    def build(d):
        part = jnp.concatenate(
            [cot[:, pl.ds(column(w, 2 * d + i), half)] for w in range(2) for i in range(2)], axis=1
        )
        placed = dot(place6[...], part, 0).astype(BF)
        stacked = jnp.concatenate(
            [
                jnp.concatenate(
                    [
                        placed[g * rows : (g + 1) * rows, c * lanes : (c + 1) * lanes]
                        for c in range(GROUP)
                    ],
                    axis=0,
                )
                for g in range(groups)
            ],
            axis=1,
        )
        out = dot(swap[...], stacked).astype(BF)
        for g in range(groups):
            send[d, g * block : (g + 1) * block, :] = out[:, g * lanes : (g + 1) * lanes]

    def gate_copy(peer):
        return pltpu.make_async_remote_copy(
            src_ref=gate_send.at[pl.ds(pl.multiple_of(peer * 8, 8), 8)],
            dst_ref=gate_recv.at[pl.ds(pl.multiple_of(me * 8, 8), 8)],
            send_sem=gate_ssem, recv_sem=gate_rsem,
            device_id=(rep, peer), device_id_type=MESH,
        )

    def router_copy(peer):
        return pltpu.make_async_remote_copy(
            src_ref=router_send.at[pl.ds(pl.multiple_of(peer * 8, 8), 8)],
            dst_ref=router_recv.at[pl.ds(pl.multiple_of(me * 8, 8), 8)],
            send_sem=router_ssem, recv_sem=router_rsem,
            device_id=(rep, peer), device_id_type=MESH,
        )

    def row_copy(d, peer):
        return pltpu.make_async_remote_copy(
            src_ref=send.at[d, pl.ds(pl.multiple_of(peer * msg, msg), msg)],
            dst_ref=recv.at[d, pl.ds(pl.multiple_of(me * msg, msg), msg)],
            send_sem=send_sem.at[d], recv_sem=recv_sem.at[d],
            device_id=(rep, peer), device_id_type=MESH,
        )

    def wait_all(buffer, size, sem):
        part = buffer.at[pl.ds(0, (peers - 1) * size)]
        pltpu.make_async_copy(part, part, sem).wait()

    build(0)
    pl.semaphore_wait(barrier, peers - 1 + 2 + nx - 1)

    @pl.loop(1, peers)
    def _(i):
        gate_copy((me + i) % peers).start()

    @pl.loop(0, steps)
    def _(d):
        @pl.when(d > 0)
        def _():
            build(d)

        @pl.loop(1, peers)
        def _(i):
            row_copy(d, (me + i) % peers).start()

        mine = pl.ds(pl.multiple_of(me * msg, msg), msg)
        recv[d, mine, :] = send[d, mine, :]

    mine8 = pl.ds(pl.multiple_of(me * 8, 8), 8)
    gate_recv[mine8, :] = gate_send[mine8, :]

    g = saved[:, :width].astype(F32)
    u = saved[:, width:].astype(F32)
    hidden[...] = g * jax.nn.sigmoid(g) * u
    ring_recv[:, 0] = jnp.zeros(ring_recv.shape[:1] + ring_recv.shape[2:], BF)
    pulled[...] = jnp.zeros_like(pulled)

    wait_all(gate_recv, 8, gate_rsem)
    scale[...] = dot(select[...].astype(BF), gate_recv[...].astype(BF))[:, :1]
    scaled[...] = (scale[...] * hidden[...]).astype(BF)
    weight_copy.wait()

    def ring_copy(which, k, s):
        return pltpu.make_async_remote_copy(
            src_ref=ring_send.at[which, k, s],
            dst_ref=ring_recv.at[which, k + 1, s],
            send_sem=ring_ssem.at[which, k, s], recv_sem=ring_rsem.at[which, k, s],
            device_id=((left if which else right), me), device_id_type=MESH,
        )

    def term(d, i, which, s):
        at = (2 * which + i) * half
        return dot(arrived[d, :, at : at + half], scaled[:, s * sub_w : (s + 1) * sub_w], 0)

    def ring_step(d, i):
        k = 2 * d + i
        for s in range(SUBS):
            for which in range(2):
                own = term(d, i, which, s)
                if i == 1:
                    ring_copy(which, k - 1, s).wait_recv()
                else:

                    @pl.when(k > 0)
                    def _():
                        ring_copy(which, k - 1, s).wait_recv()

                ring_send[which, k, s] = (own + ring_recv[which, k, s].astype(F32)).astype(BF)
                ring_copy(which, k, s).start()

    @pl.loop(0, steps)
    def _(d):
        wait_all(recv.at[d], msg, recv_sem.at[d])
        stacked = jnp.concatenate(
            [recv[d, g * block : (g + 1) * block, :] for g in range(groups)], axis=1
        )
        out = dot(swap[...], stacked).astype(BF)
        for g in range(groups):
            for c in range(GROUP):
                arrived[d, g * rows : (g + 1) * rows, c * lanes : (c + 1) * lanes] = out[
                    c * rows : (c + 1) * rows, g * lanes : (g + 1) * lanes
                ]
        ring_step(d, 0)
        total = pulled[...]
        for w in range(2):
            for i in range(2):
                at = (2 * w + i) * half
                total = total + dot(
                    arrived[d, :, at : at + half], weight[pl.ds(column(w, 2 * d + i), half), :]
                )
        pulled[...] = total

        @pl.when(d < steps - 1)
        def _():
            ring_step(d, 1)

    router = jnp.sum(pulled[...] * hidden[...], axis=1, keepdims=True)
    router_send[...] = dot(
        select[...], jnp.broadcast_to(router, (slots, 128)), 0, precision=lax.Precision.HIGHEST
    )

    @pl.loop(1, peers)
    def _(i):
        router_copy((me + i) % peers).start()

    router_recv[mine8, :] = router_send[mine8, :]
    g = saved[:, :width].astype(F32)
    u = saved[:, width:].astype(F32)
    sg = jax.nn.sigmoid(g)
    dh = scale[...] * pulled[...]
    pair_out[:, :width] = (dh * u * sg * (1.0 + g * (1.0 - sg))).astype(BF)
    pair_out[:, width:] = (dh * g * sg).astype(BF)

    for s in range(SUBS):
        for which in range(2):
            own = term(steps - 1, 1, which, s)
            ring_copy(which, ny - 2, s).wait_recv()
            chunk[which * half : (which + 1) * half, s * sub_w : (s + 1) * sub_w] = own + ring_recv[
                which, ny - 1, s
            ].astype(F32)
    x_send[...] = chunk[...].astype(BF)

    def x_copy(i):
        other = (xh + i) % nx
        return pltpu.make_async_remote_copy(
            src_ref=x_send.at[pl.ds(pl.multiple_of(other * out_rows, out_rows), out_rows)],
            dst_ref=x_recv.at[i - 1],
            send_sem=x_ssem.at[i - 1], recv_sem=x_rsem.at[i - 1],
            device_id=(y * nx + other, me), device_id_type=MESH,
        )

    for i in range(1, nx):
        x_copy(i).start()

    wait_all(router_recv, 8, router_rsem)
    token_out[...] = dot(place8[...], router_recv[...], precision=lax.Precision.HIGHEST)[:, :1]

    wait_all(gate_send, 8, gate_ssem)
    wait_all(router_send, 8, router_ssem)

    @pl.loop(0, steps)
    def _(d):
        wait_all(send.at[d], msg, send_sem.at[d])

    @pl.loop(0, ny - 1)
    def _(k):
        for which in range(2):
            for s in range(SUBS):
                ring_copy(which, k, s).wait_send()

    grad = chunk[pl.ds(pl.multiple_of(xh * out_rows, out_rows), out_rows), :]
    for i in range(1, nx):
        x_copy(i).wait_recv()
        grad = grad + x_recv[i - 1].astype(F32)
    grad_out[...] = grad
    for i in range(1, nx):
        x_copy(i).wait_send()


def shards(nx, cotangent, routes, gate_weight, down_weight, saved_pre):
    peers = lax.axis_size("exp")
    ny = lax.axis_size("rep") // nx
    tokens, model = cotangent.shape
    slots, double = saved_pre.shape[2:]
    width = double // 2
    half = model // ny // 2
    steps = ny // 2
    out_rows = model // (ny * nx)
    msg = GROUP * CAP
    block = GROUP * msg
    vmem = pl.BlockSpec(memory_space=pltpu.VMEM)
    dma = pltpu.SemaphoreType.DMA
    grad, pairs, token = pl.pallas_call(
        functools.partial(kernel, ny, nx, peers),
        out_shape=(
            jax.ShapeDtypeStruct((out_rows, width), F32),
            jax.ShapeDtypeStruct((slots, double), BF),
            jax.ShapeDtypeStruct((tokens, 1), F32),
        ),
        in_specs=[vmem, vmem, vmem, pl.BlockSpec(memory_space=pl.ANY), vmem],
        out_specs=(vmem, vmem, vmem),
        scratch_shapes=[
            pltpu.VMEM((model, width), BF),
            pltpu.VMEM((steps, peers * msg, half // 2), BF),
            pltpu.VMEM((steps, peers * msg, half // 2), BF),
            pltpu.VMEM((steps, slots, 4 * half), BF),
            pltpu.VMEM((tokens, slots), BF),
            pltpu.VMEM((tokens, peers * 8), F32),
            pltpu.VMEM((block, block), BF),
            pltpu.VMEM((slots, peers * 8), F32),
            pltpu.VMEM((peers * 8, 128), F32),
            pltpu.VMEM((peers * 8, 128), F32),
            pltpu.VMEM((peers * 8, 128), F32),
            pltpu.VMEM((peers * 8, 128), F32),
            pltpu.VMEM((slots, width), F32),
            pltpu.VMEM((slots, 1), F32),
            pltpu.VMEM((slots, width), BF),
            pltpu.VMEM((slots, width), F32),
            pltpu.VMEM((2, ny - 1, SUBS, half, width // SUBS), BF),
            pltpu.VMEM((2, ny, SUBS, half, width // SUBS), BF),
            pltpu.VMEM((2 * half, width), F32),
            pltpu.VMEM((2 * half, width), BF),
            pltpu.VMEM((nx - 1, out_rows, width), BF),
            dma, dma((steps,)), dma((steps,)), dma, dma, dma, dma,
            dma((2, ny - 1, SUBS)), dma((2, ny - 1, SUBS)), dma((nx - 1,)), dma((nx - 1,)),
        ],
        compiler_params=pltpu.CompilerParams(
            collective_id=0, has_side_effects=True, vmem_limit_bytes=56 * 1024 * 1024
        ),
        cost_estimate=pl.CostEstimate(
            flops=4 * slots * model * width, bytes_accessed=12 * 1024 * 1024, transcendentals=0
        ),
        name="expert_backward",
    )(cotangent, routes, gate_weight, down_weight[0], saved_pre[0, 0])
    return grad[None], pairs[None, None], token


def solution(mesh):
    nx = 4 if mesh.shape["rep"] == 32 else 2
    in_specs = (
        P(("rep", "exp"), None),
        P(("rep", "exp"), None),
        P(("rep", "exp"), None),
        P("exp", None, None),
        P("rep", "exp", None, None),
    )
    out_specs = (P("exp", "rep", None), P("rep", "exp", None, None), P(("rep", "exp"), None))
    return jax.shard_map(
        functools.partial(shards, nx), mesh=mesh, in_specs=in_specs, out_specs=out_specs,
        check_vma=False,
    )
```

```python
import functools

import jax
import jax.numpy as jnp
from jax import lax
from jax.experimental import pallas as pl
from jax.experimental.pallas import tpu as pltpu
from jax.sharding import PartitionSpec as P

MESH = pl.DeviceIdType.MESH
BF = jnp.bfloat16
F32 = jnp.float32
CAP = 6
GROUP = 8
WIDTHS = (384, 256, 128)


def dot(a, b, lhs=1, **kw):
    return lax.dot_general(a, b, (((lhs,), (0,)), ((), ())), preferred_element_type=F32, **kw)


def iota(shape, dim):
    return lax.broadcasted_iota(jnp.int32, shape, dim).astype(F32)


def kernel(
    ny, nx, peers, widths,
    cot, routes, gate, weight_hbm, saved,
    grad_out, pair_out, token_out,
    weight, send, recv, edge_send, edge_recv, arrived, place6, place8, swap, edge, pick, select,
    router_send, router_recv, hidden, scale, scaled, pulled,
    ring_send0, ring_recv0, ring_send1, ring_recv1, chunk, x_send0, x_recv0, x_send1, x_recv1,
    cross_send, cross_recv, column_send, column_recv,
    weight_sem, send_sem, recv_sem, edge_ssem, edge_rsem, router_ssem, router_rsem,
    ring_ssem, ring_rsem, x_ssem, x_rsem, cross_ssem, cross_rsem, column_ssem, column_rsem,
):
    tokens = cot.shape[0]
    slots = peers * CAP
    groups = peers // GROUP
    width = weight.shape[1]
    span = cot.shape[1] // ny
    half = span // 2
    rows = GROUP * CAP
    block = GROUP * rows
    msg = GROUP * CAP
    lanes = 128
    piece = half // nx
    ring_send, ring_recv = (ring_send0, ring_send1), (ring_recv0, ring_recv1)
    x_send, x_recv = (x_send0, x_send1), (x_recv0, x_recv1)
    starts = (0, widths[0], widths[0] + widths[1])
    cross_at = starts[2]
    last = ny - 1
    rep, me = lax.axis_index("rep"), lax.axis_index("exp")
    y, xh = rep // nx, rep % nx
    right = ((y + 1) % ny) * nx + xh
    left = ((y + ny - 1) % ny) * nx + xh

    weight_copy = pltpu.make_async_copy(weight_hbm, weight, weight_sem)
    weight_copy.start()

    barrier = pltpu.get_barrier_semaphore()

    @pl.loop(1, peers)
    def _(i):
        pl.semaphore_signal(
            barrier, inc=1, device_id=(rep, (me + i) % peers), device_id_type=MESH
        )

    for other in (left, right):
        pl.semaphore_signal(barrier, inc=1, device_id=(other, me), device_id_type=MESH)
    for i in range(1, nx):
        pl.semaphore_signal(
            barrier, inc=1, device_id=(y * nx + (xh + i) % nx, me), device_id_type=MESH
        )

    def chunk_at(which, k):
        return (y + ny - 1 - k) % ny if which == 0 else (y + 1 + k) % ny

    eye = iota((tokens, tokens), 0) == iota((tokens, tokens), 1)

    def as_column(row):
        return jnp.sum(jnp.where(eye, row, 0.0), axis=1, keepdims=True)

    ids = as_column(routes[...].astype(F32))
    one_hot = ids == iota((tokens, peers), 1)
    below = (iota((tokens, tokens), 0) > iota((tokens, tokens), 1)).astype(F32).astype(BF)
    earlier = dot(below, one_hot.astype(F32).astype(BF))
    position = jnp.sum(jnp.where(one_hot, earlier, 0.0), axis=1, keepdims=True)
    place6[...] = (ids * CAP + position == iota((tokens, slots), 1)).astype(F32).astype(BF)
    place8[...] = (ids * 8 + position == iota((tokens, peers * 8), 1)).astype(F32)
    gates = jnp.broadcast_to(as_column(gate[...]), (tokens, lanes)).astype(BF)

    r = iota((block, 1), 0)
    a = jnp.floor((r + 0.5) * (1.0 / rows))
    ab = jnp.floor((r + 0.5) * (1.0 / CAP))
    source = (ab - GROUP * a) * rows + a * CAP + (r - CAP * ab)
    swap[...] = (source == iota((block, block), 1)).astype(F32).astype(BF)
    r = iota((GROUP * 32, 1), 0)
    a = jnp.floor((r + 0.5) * (1.0 / 32))
    m = r - 32 * a
    b = jnp.floor((m + 0.5) * (1.0 / CAP))
    source = b * rows + a * CAP + (m - CAP * b)
    edge[...] = (source == iota((GROUP * 32, 5 * rows), 1)).astype(F32).astype(BF)
    for which in range(2):
        r = iota((half, half), 1)
        owner = jnp.floor((r + 0.5) * (1.0 / piece))
        source = r + piece * (owner + which)
        for q in range(2):
            pick[which, q * half : (q + 1) * half, :] = (
                (iota((half, half), 0) + q * half == source).astype(F32).astype(BF)
            )
    r = iota((slots, 1), 0)
    spread = r + (8 - CAP) * jnp.floor((r + 0.5) * (1.0 / CAP))
    select[...] = (spread == iota((slots, peers * 8), 1)).astype(F32)

    def half_columns(which, k):
        at = pl.multiple_of(chunk_at(which, k) * span, span)
        return dot(cot[:, pl.ds(at, span)], pick[which]).astype(BF)

    def arrange(matrix, parts):
        placed = dot(place6[...], jnp.concatenate(parts, axis=1), 0).astype(BF)
        count = placed.shape[1] // lanes
        stacked = [
            [placed[g * rows : (g + 1) * rows, c * lanes : (c + 1) * lanes] for c in range(count)]
            for g in range(groups)
        ]
        stacked = jnp.concatenate([jnp.concatenate(s, axis=0) for s in stacked], axis=1)
        return dot(matrix, stacked).astype(BF)

    def build(d):
        out = arrange(
            swap[...], [half_columns(w, 2 * d + 1 + i) for i in range(2) for w in range(2)]
        )
        for g in range(groups):
            send[d, g * block : (g + 1) * block, :] = out[:, g * lanes : (g + 1) * lanes]

    def build_edge(e, k):
        out = arrange(edge[...], [half_columns(w, k) for w in range(2)] + [gates])
        size = GROUP * 32
        for g in range(groups):
            edge_send[e, g * size : (g + 1) * size, :] = out[:, g * lanes : (g + 1) * lanes]

    def router_copy(peer):
        return pltpu.make_async_remote_copy(
            src_ref=router_send.at[pl.ds(pl.multiple_of(peer * 8, 8), 8)],
            dst_ref=router_recv.at[pl.ds(pl.multiple_of(me * 8, 8), 8)],
            send_sem=router_ssem, recv_sem=router_rsem,
            device_id=(rep, peer), device_id_type=MESH,
        )

    def row_copy(d, peer):
        return pltpu.make_async_remote_copy(
            src_ref=send.at[d, pl.ds(pl.multiple_of(peer * msg, msg), msg)],
            dst_ref=recv.at[d, pl.ds(pl.multiple_of(me * msg, msg), msg)],
            send_sem=send_sem.at[d], recv_sem=recv_sem.at[d],
            device_id=(rep, peer), device_id_type=MESH,
        )

    def edge_copy(e, peer):
        return pltpu.make_async_remote_copy(
            src_ref=edge_send.at[e, pl.ds(pl.multiple_of(peer * 32, 32), 32)],
            dst_ref=edge_recv.at[e, pl.ds(pl.multiple_of(me * 32, 32), 32)],
            send_sem=edge_ssem.at[e], recv_sem=edge_rsem.at[e],
            device_id=(rep, peer), device_id_type=MESH,
        )

    def to_peers(copy):
        @pl.loop(1, peers)
        def _(i):
            copy((me + i) % peers).start()

    def wait_all(buffer, size, sem):
        part = buffer.at[pl.ds(0, (peers - 1) * size)]
        pltpu.make_async_copy(part, part, sem).wait()

    build_edge(0, 0)
    pl.semaphore_wait(barrier, peers - 1 + 2 + nx - 1)
    to_peers(lambda peer: edge_copy(0, peer))
    mine = pl.ds(pl.multiple_of(me * msg, msg), msg)
    mine32 = pl.ds(pl.multiple_of(me * 32, 32), 32)
    mine8 = pl.ds(pl.multiple_of(me * 8, 8), 8)
    edge_recv[0, mine32, :] = edge_send[0, mine32, :]

    @pl.loop(0, last // 2)
    def _(d):
        build(d)
        recv[d, mine, :] = send[d, mine, :]

    build_edge(1, last)
    edge_recv[1, mine32, :] = edge_send[1, mine32, :]

    g = saved[:, :width].astype(F32)
    u = saved[:, width:].astype(F32)
    hidden[...] = g * jax.nn.sigmoid(g) * u
    pulled[...] = jnp.zeros_like(pulled)
    weight_copy.wait()

    def take_edge(e, k):
        wait_all(edge_recv.at[e], 32, edge_rsem.at[e])
        size = GROUP * 32
        stacked = jnp.concatenate(
            [edge_recv[e, g * size : (g + 1) * size, :] for g in range(groups)], axis=1
        )
        out = dot(edge[...], stacked, 0)
        for g in range(groups):
            for c in range(4):
                arrived[k, g * rows : (g + 1) * rows, c * lanes : (c + 1) * lanes] = out[
                    c * rows : (c + 1) * rows, g * lanes : (g + 1) * lanes
                ].astype(BF)
        return out

    def take(d):
        wait_all(recv.at[d], msg, recv_sem.at[d])
        stacked = jnp.concatenate(
            [recv[d, g * block : (g + 1) * block, :] for g in range(groups)], axis=1
        )
        out = dot(swap[...], stacked).astype(BF)
        for g in range(groups):
            for c in range(GROUP):
                at = c % 4 * lanes
                arrived[2 * d + 1 + c // 4, g * rows : (g + 1) * rows, at : at + lanes] = out[
                    c * rows : (c + 1) * rows, g * lanes : (g + 1) * lanes
                ]

    def ring_copy(which, k, s):
        return pltpu.make_async_remote_copy(
            src_ref=ring_send[s].at[which, k], dst_ref=ring_recv[s].at[which, k],
            send_sem=ring_ssem.at[which, k, s], recv_sem=ring_rsem.at[which, k, s],
            device_id=((left if which else right), me), device_id_type=MESH,
        )

    def column_copy(which, k):
        return pltpu.make_async_remote_copy(
            src_ref=column_send.at[which, k], dst_ref=column_recv.at[which, k],
            send_sem=column_ssem.at[which, k], recv_sem=column_rsem.at[which, k],
            device_id=((left if which else right), me), device_id_type=MESH,
        )

    def cross_copy(which, k, i):
        other = (xh + i) % nx
        return pltpu.make_async_remote_copy(
            src_ref=cross_send.at[which, k, pl.ds(pl.multiple_of(other * piece, piece), piece)],
            dst_ref=cross_recv.at[which, k, i - 1],
            send_sem=cross_ssem.at[which, k, i - 1], recv_sem=cross_rsem.at[which, k, i - 1],
            device_id=(y * nx + other, me), device_id_type=MESH,
        )

    def x_copy(which, s, i):
        other = (xh + i) % nx
        return pltpu.make_async_remote_copy(
            src_ref=x_send[s].at[which, pl.ds(pl.multiple_of(other * piece, piece), piece)],
            dst_ref=x_recv[s].at[which, i - 1],
            send_sem=x_ssem.at[which, s, i - 1], recv_sem=x_rsem.at[which, s, i - 1],
            device_id=(y * nx + other, me), device_id_type=MESH,
        )

    def term(k, which, at, size):
        part = arrived[k, :, which * half : (which + 1) * half]
        return dot(part, scaled[:, at : at + size], 0)

    def ring_sum(k, which, s, first=False):
        own = term(k, which, starts[s], widths[s])
        if not first:
            ring_copy(which, k - 1, s).wait_recv()
            own = own + ring_recv[s][which, k - 1].astype(F32)
        return own

    def ring_step(k, first=False):
        for s in range(2):
            for which in range(2):
                ring_send[s][which, k] = ring_sum(k, which, s, first).astype(BF)
                ring_copy(which, k, s).start()

    def cross_step(k):
        for which in range(2):
            cross_send[which, k] = term(k, which, cross_at, widths[2]).astype(BF)
            for i in range(1, nx):
                cross_copy(which, k, i).start()

    own_piece = pl.ds(pl.multiple_of(xh * piece, piece), piece)

    def column_step(k, first=False, final=False):
        for which in range(2):
            total = cross_send[which, k, own_piece, :].astype(F32)
            for i in range(1, nx):
                cross_copy(which, k, i).wait_recv()
                total = total + cross_recv[which, k, i - 1].astype(F32)
            if not first:
                column_copy(which, k - 1).wait_recv()
                total = total + column_recv[which, k - 1].astype(F32)
            if final:
                grad_out[which * piece : (which + 1) * piece, cross_at:] = total
            else:
                column_send[which, k] = total.astype(BF)
                column_copy(which, k).start()

    def pull(k):
        total = pulled[...]
        for w in range(2):
            at = chunk_at(w, k) * span + w * piece
            part = jnp.concatenate(
                [
                    weight[pl.ds(pl.multiple_of(at + 2 * piece * q, piece), piece), :]
                    for q in range(nx)
                ],
                axis=0,
            )
            total = total + dot(arrived[k, :, w * half : (w + 1) * half], part)
        pulled[...] = total

    out = take_edge(0, 0)
    for g in range(groups):
        scale[g * rows : (g + 1) * rows, :] = out[4 * rows :, g * lanes : (g + 1) * lanes]
    scaled[...] = (scale[:, :1] * hidden[...]).astype(BF)
    ring_step(0, first=True)
    cross_step(0)
    to_peers(lambda peer: row_copy(0, peer))
    pull(0)

    def pair_of_steps(d, first):
        take(d)
        k = 2 * d + 1
        ring_step(k)
        cross_step(k)
        column_step(k - 1, first)

        if first:
            to_peers(lambda peer: row_copy(1, peer))
        else:

            @pl.when(d < last // 2 - 1)
            def _():
                to_peers(lambda peer: row_copy(d + 1, peer))

            @pl.when(d == last // 2 - 1)
            def _():
                to_peers(lambda peer: edge_copy(1, peer))

        cross_step(k + 1)
        pull(k)
        pull(k + 1)
        ring_step(k + 1)
        column_step(k)

    pair_of_steps(0, True)

    @pl.loop(1, last // 2)
    def _(d):
        pair_of_steps(d, False)

    take_edge(1, last)
    cross_step(last)
    pull(last)

    router = jnp.sum(pulled[...] * hidden[...], axis=1, keepdims=True)
    router_send[...] = dot(
        select[...], jnp.broadcast_to(router, (slots, lanes)), 0, precision=lax.Precision.HIGHEST
    )
    to_peers(router_copy)
    router_recv[mine8, :] = router_send[mine8, :]
    column_step(last - 1)
    g = saved[:, :width].astype(F32)
    u = saved[:, width:].astype(F32)
    sg = jax.nn.sigmoid(g)
    dh = scale[:, :1] * pulled[...]
    pair_out[:, :width] = (dh * u * sg * (1.0 + g * (1.0 - sg))).astype(BF)
    pair_out[:, width:] = (dh * g * sg).astype(BF)

    for s in range(2):
        for which in range(2):
            own = ring_sum(last, which, s)
            chunk[which, :, starts[s] : starts[s + 1]] = own
            x_send[s][which] = own.astype(BF)
            for i in range(1, nx):
                x_copy(which, s, i).start()

    column_step(last, final=True)
    wait_all(router_recv, 8, router_rsem)
    token = dot(place8[...], router_recv[...], precision=lax.Precision.HIGHEST)
    token_out[...] = jnp.sum(jnp.where(eye, token, 0.0), axis=0, keepdims=True)

    wait_all(router_send, 8, router_ssem)
    for e in range(2):
        wait_all(edge_send.at[e], 32, edge_ssem.at[e])

    @pl.loop(0, last // 2)
    def _(d):
        wait_all(send.at[d], msg, send_sem.at[d])

    @pl.loop(0, last)
    def _(k):
        for which in range(2):
            column_copy(which, k).wait_send()
            for s in range(2):
                ring_copy(which, k, s).wait_send()

    @pl.loop(0, ny)
    def _(k):
        for which in range(2):
            for i in range(1, nx):
                cross_copy(which, k, i).wait_send()

    for s in range(2):
        for which in range(2):
            total = chunk[which, own_piece, starts[s] : starts[s + 1]]
            for i in range(1, nx):
                x_copy(which, s, i).wait_recv()
                total = total + x_recv[s][which, i - 1].astype(F32)
            grad_out[which * piece : (which + 1) * piece, starts[s] : starts[s + 1]] = total
            for i in range(1, nx):
                x_copy(which, s, i).wait_send()


def shards(nx, widths, cotangent, routes, gate_weight, down_weight, saved_pre):
    peers = lax.axis_size("exp")
    ny = lax.axis_size("rep") // nx
    tokens, model = cotangent.shape
    slots, double = saved_pre.shape[2:]
    width = double // 2
    half = model // ny // 2
    last = ny - 1
    pairs = last // 2
    piece = half // nx
    msg = GROUP * CAP
    block = GROUP * msg
    vmem = pl.BlockSpec(memory_space=pltpu.VMEM)
    dma = pltpu.SemaphoreType.DMA
    wa, wb, wc = widths
    grad, pair, token = pl.pallas_call(
        functools.partial(kernel, ny, nx, peers, widths),
        out_shape=(
            jax.ShapeDtypeStruct((2 * piece, width), F32),
            jax.ShapeDtypeStruct((slots, double), BF),
            jax.ShapeDtypeStruct((1, tokens), F32),
        ),
        in_specs=[vmem, vmem, vmem, pl.BlockSpec(memory_space=pl.ANY), vmem],
        out_specs=(vmem, vmem, vmem),
        scratch_shapes=[
            pltpu.VMEM((model, width), BF),
            pltpu.VMEM((pairs, peers * msg, 128), BF),
            pltpu.VMEM((pairs, peers * msg, 128), BF),
            pltpu.VMEM((2, peers * 32, 128), BF),
            pltpu.VMEM((2, peers * 32, 128), BF),
            pltpu.VMEM((ny, slots, 2 * half), BF),
            pltpu.VMEM((tokens, slots), BF),
            pltpu.VMEM((tokens, peers * 8), F32),
            pltpu.VMEM((block, block), BF),
            pltpu.VMEM((GROUP * 32, 5 * msg), BF),
            pltpu.VMEM((2, 2 * half, half), BF),
            pltpu.VMEM((slots, peers * 8), F32),
            pltpu.VMEM((peers * 8, 128), F32),
            pltpu.VMEM((peers * 8, 128), F32),
            pltpu.VMEM((slots, width), F32),
            pltpu.VMEM((slots, 128), F32),
            pltpu.VMEM((slots, width), BF),
            pltpu.VMEM((slots, width), F32),
            pltpu.VMEM((2, last, half, wa), BF),
            pltpu.VMEM((2, last, half, wa), BF),
            pltpu.VMEM((2, last, half, wb), BF),
            pltpu.VMEM((2, last, half, wb), BF),
            pltpu.VMEM((2, half, wa + wb), F32),
            pltpu.VMEM((2, half, wa), BF),
            pltpu.VMEM((2, nx - 1, piece, wa), BF),
            pltpu.VMEM((2, half, wb), BF),
            pltpu.VMEM((2, nx - 1, piece, wb), BF),
            pltpu.VMEM((2, ny, half, wc), BF),
            pltpu.VMEM((2, ny, nx - 1, piece, wc), BF),
            pltpu.VMEM((2, last, piece, wc), BF),
            pltpu.VMEM((2, last, piece, wc), BF),
            dma, dma((pairs,)), dma((pairs,)), dma((2,)), dma((2,)), dma, dma,
            dma((2, last, 2)), dma((2, last, 2)), dma((2, 2, nx - 1)), dma((2, 2, nx - 1)),
            dma((2, ny, nx - 1)), dma((2, ny, nx - 1)), dma((2, last)), dma((2, last)),
        ],
        compiler_params=pltpu.CompilerParams(
            collective_id=0, has_side_effects=True, vmem_limit_bytes=56 * 1024 * 1024
        ),
        cost_estimate=pl.CostEstimate(
            flops=4 * slots * model * width, bytes_accessed=12 * 1024 * 1024, transcendentals=0
        ),
        name="expert_backward",
    )(
        cotangent,
        routes.reshape(1, tokens),
        gate_weight.reshape(1, tokens),
        down_weight[0],
        saved_pre[0, 0],
    )
    return grad[None], pair[None, None], token.reshape(tokens, 1)


def solution(mesh):
    nx = 4 if mesh.shape["rep"] == 32 else 2
    in_specs = (
        P(("rep", "exp"), None),
        P(("rep", "exp"), None),
        P(("rep", "exp"), None),
        P("exp", None, None),
        P("rep", "exp", None, None),
    )
    out_specs = (P("exp", "rep", None), P("rep", "exp", None, None), P(("rep", "exp"), None))
    return jax.shard_map(
        functools.partial(shards, nx, WIDTHS), mesh=mesh, in_specs=in_specs, out_specs=out_specs,
        check_vma=False,
    )
```

```python
import functools

import jax
import jax.numpy as jnp
from jax import lax
from jax.experimental import pallas as pl
from jax.experimental.pallas import tpu as pltpu
from jax.sharding import PartitionSpec as P

MESH = pl.DeviceIdType.MESH
BF = jnp.bfloat16
F32 = jnp.float32
CAP = 6
GROUP = 8
SUB = 128
CROSS = 128
AHEAD = 3
LAG = 2


def dot(a, b, lhs=1, **kw):
    return lax.dot_general(a, b, (((lhs,), (0,)), ((), ())), preferred_element_type=F32, **kw)


def iota(shape, dim):
    return lax.broadcasted_iota(jnp.int32, shape, dim).astype(F32)


def kernel(
    ny, nx, peers,
    cot, routes, gate, weight_hbm, saved,
    grad_out, pair_out, token_out,
    weight, send, recv, edge_send, edge_recv, arrived, place6, place8, swap, edge, pick, select,
    router_send, router_recv, hidden, scale, scaled, pulled,
    own, ring_send, ring_recv, chunk, x_send, x_recv,
    cross_send, cross_recv, column_send, column_recv,
    weight_sem, send_sem, recv_sem, edge_ssem, edge_rsem, router_ssem, router_rsem,
    ring_ssem, ring_rsem, x_ssem, x_rsem, cross_ssem, cross_rsem, column_ssem, column_rsem,
):
    tokens = cot.shape[0]
    slots = peers * CAP
    groups = peers // GROUP
    width = weight.shape[1]
    span = cot.shape[1] // ny
    half = span // 2
    rows = GROUP * CAP
    block = GROUP * rows
    msg = GROUP * CAP
    lanes = 128
    piece = half // nx
    cross_at = width - CROSS
    subs = cross_at // SUB
    last = ny - 1
    rep, me = lax.axis_index("rep"), lax.axis_index("exp")
    y, xh = rep // nx, rep % nx
    right = ((y + 1) % ny) * nx + xh
    left = ((y + ny - 1) % ny) * nx + xh

    weight_copy = pltpu.make_async_copy(weight_hbm, weight, weight_sem)
    weight_copy.start()

    barrier = pltpu.get_barrier_semaphore()

    @pl.loop(1, peers)
    def _(i):
        pl.semaphore_signal(
            barrier, inc=1, device_id=(rep, (me + i) % peers), device_id_type=MESH
        )

    for other in (left, right):
        pl.semaphore_signal(barrier, inc=1, device_id=(other, me), device_id_type=MESH)
    for i in range(1, nx):
        pl.semaphore_signal(
            barrier, inc=1, device_id=(y * nx + (xh + i) % nx, me), device_id_type=MESH
        )

    def chunk_at(which, k):
        return (y + ny - 1 - k) % ny if which == 0 else (y + 1 + k) % ny

    eye = iota((tokens, tokens), 0) == iota((tokens, tokens), 1)

    def as_column(row):
        return jnp.sum(jnp.where(eye, row, 0.0), axis=1, keepdims=True)

    ids = as_column(routes[...].astype(F32))
    one_hot = ids == iota((tokens, peers), 1)
    below = (iota((tokens, tokens), 0) > iota((tokens, tokens), 1)).astype(F32).astype(BF)
    earlier = dot(below, one_hot.astype(F32).astype(BF))
    position = jnp.sum(jnp.where(one_hot, earlier, 0.0), axis=1, keepdims=True)
    place6[...] = (ids * CAP + position == iota((tokens, slots), 1)).astype(F32).astype(BF)
    gates = jnp.broadcast_to(as_column(gate[...]), (tokens, lanes)).astype(BF)

    r = iota((GROUP * 32, 1), 0)
    a = jnp.floor((r + 0.5) * (1.0 / 32))
    m = r - 32 * a
    b = jnp.floor((m + 0.5) * (1.0 / CAP))
    source = b * rows + a * CAP + (m - CAP * b)
    edge[...] = (source == iota((GROUP * 32, 5 * rows), 1)).astype(F32).astype(BF)
    for which in range(2):
        r = iota((half, half), 1)
        owner = jnp.floor((r + 0.5) * (1.0 / piece))
        source = r + piece * (owner + which)
        for q in range(2):
            pick[which, q * half : (q + 1) * half, :] = (
                (iota((half, half), 0) + q * half == source).astype(F32).astype(BF)
            )
    def half_columns(which, k):
        at = pl.multiple_of(chunk_at(which, k) * span, span)
        return dot(cot[:, pl.ds(at, span)], pick[which]).astype(BF)

    def arrange(matrix, parts):
        placed = dot(place6[...], jnp.concatenate(parts, axis=1), 0).astype(BF)
        count = placed.shape[1] // lanes
        stacked = [
            [placed[g * rows : (g + 1) * rows, c * lanes : (c + 1) * lanes] for c in range(count)]
            for g in range(groups)
        ]
        stacked = jnp.concatenate([jnp.concatenate(s, axis=0) for s in stacked], axis=1)
        return dot(matrix, stacked).astype(BF)

    def build(d):
        out = arrange(
            swap[...], [half_columns(w, 2 * d + 1 + i) for i in range(2) for w in range(2)]
        )
        for g in range(groups):
            send[d, g * block : (g + 1) * block, :] = out[:, g * lanes : (g + 1) * lanes]

    def build_edge(e, k):
        out = arrange(edge[...], [half_columns(w, k) for w in range(2)] + [gates])
        size = GROUP * 32
        for g in range(groups):
            edge_send[e, g * size : (g + 1) * size, :] = out[:, g * lanes : (g + 1) * lanes]

    def router_copy(peer):
        return pltpu.make_async_remote_copy(
            src_ref=router_send.at[pl.ds(pl.multiple_of(peer * 8, 8), 8)],
            dst_ref=router_recv.at[pl.ds(pl.multiple_of(me * 8, 8), 8)],
            send_sem=router_ssem, recv_sem=router_rsem,
            device_id=(rep, peer), device_id_type=MESH,
        )

    def row_copy(d, peer):
        return pltpu.make_async_remote_copy(
            src_ref=send.at[d, pl.ds(pl.multiple_of(peer * msg, msg), msg)],
            dst_ref=recv.at[d, pl.ds(pl.multiple_of(me * msg, msg), msg)],
            send_sem=send_sem.at[d], recv_sem=recv_sem.at[d],
            device_id=(rep, peer), device_id_type=MESH,
        )

    def edge_copy(e, peer):
        return pltpu.make_async_remote_copy(
            src_ref=edge_send.at[e, pl.ds(pl.multiple_of(peer * 32, 32), 32)],
            dst_ref=edge_recv.at[e, pl.ds(pl.multiple_of(me * 32, 32), 32)],
            send_sem=edge_ssem.at[e], recv_sem=edge_rsem.at[e],
            device_id=(rep, peer), device_id_type=MESH,
        )

    def to_peers(copy):
        @pl.loop(1, peers)
        def _(i):
            off = (i % 2) * ((i + 1) // 2) + ((i + 1) % 2) * (peers - i // 2)
            copy((me + off) % peers).start()

    def wait_all(buffer, size, sem):
        part = buffer.at[pl.ds(0, (peers - 1) * size)]
        pltpu.make_async_copy(part, part, sem).wait()

    build_edge(0, 0)
    pl.semaphore_wait(barrier, peers - 1 + 2 + nx - 1)
    to_peers(lambda peer: edge_copy(0, peer))
    mine = pl.ds(pl.multiple_of(me * msg, msg), msg)
    mine32 = pl.ds(pl.multiple_of(me * 32, 32), 32)
    mine8 = pl.ds(pl.multiple_of(me * 8, 8), 8)
    edge_recv[0, mine32, :] = edge_send[0, mine32, :]

    r = iota((block, 1), 0)
    a = jnp.floor((r + 0.5) * (1.0 / rows))
    ab = jnp.floor((r + 0.5) * (1.0 / CAP))
    source = (ab - GROUP * a) * rows + a * CAP + (r - CAP * ab)
    swap[...] = (source == iota((block, block), 1)).astype(F32).astype(BF)
    place8[...] = (ids * 8 + position == iota((tokens, peers * 8), 1)).astype(F32)
    r = iota((slots, 1), 0)
    spread = r + (8 - CAP) * jnp.floor((r + 0.5) * (1.0 / CAP))
    select[...] = (spread == iota((slots, peers * 8), 1)).astype(F32)

    @pl.loop(0, last // 2)
    def _(d):
        build(d)
        recv[d, mine, :] = send[d, mine, :]

    to_peers(lambda peer: row_copy(0, peer))
    build_edge(1, last)
    edge_recv[1, mine32, :] = edge_send[1, mine32, :]

    g = saved[:, :width].astype(F32)
    u = saved[:, width:].astype(F32)
    hidden[...] = g * jax.nn.sigmoid(g) * u
    pulled[...] = jnp.zeros_like(pulled)
    weight_copy.wait()

    def take_edge(e, k):
        wait_all(edge_recv.at[e], 32, edge_rsem.at[e])
        size = GROUP * 32
        stacked = jnp.concatenate(
            [edge_recv[e, g * size : (g + 1) * size, :] for g in range(groups)], axis=1
        )
        out = dot(edge[...], stacked, 0)
        for g in range(groups):
            for c in range(4):
                arrived[k, g * rows : (g + 1) * rows, c * lanes : (c + 1) * lanes] = out[
                    c * rows : (c + 1) * rows, g * lanes : (g + 1) * lanes
                ].astype(BF)
        return out

    def take(d):
        wait_all(recv.at[d], msg, recv_sem.at[d])
        stacked = jnp.concatenate(
            [recv[d, g * block : (g + 1) * block, :] for g in range(groups)], axis=1
        )
        out = dot(swap[...], stacked).astype(BF)
        for g in range(groups):
            for c in range(GROUP):
                at = c % 4 * lanes
                arrived[2 * d + 1 + c // 4, g * rows : (g + 1) * rows, at : at + lanes] = out[
                    c * rows : (c + 1) * rows, g * lanes : (g + 1) * lanes
                ]

    def ring_copy(which, k, s):
        return pltpu.make_async_remote_copy(
            src_ref=ring_send.at[which, k, s], dst_ref=ring_recv.at[which, k, s],
            send_sem=ring_ssem.at[which, k, s], recv_sem=ring_rsem.at[which, k, s],
            device_id=((left if which else right), me), device_id_type=MESH,
        )

    def column_copy(which, k):
        return pltpu.make_async_remote_copy(
            src_ref=column_send.at[which, k], dst_ref=column_recv.at[which, k + 1],
            send_sem=column_ssem.at[which, k], recv_sem=column_rsem.at[which, k],
            device_id=((left if which else right), me), device_id_type=MESH,
        )

    def cross_copy(which, k, i):
        other = (xh + i) % nx
        return pltpu.make_async_remote_copy(
            src_ref=cross_send.at[which, k, pl.ds(pl.multiple_of(other * piece, piece), piece)],
            dst_ref=cross_recv.at[which, k, i - 1],
            send_sem=cross_ssem.at[which, k, i - 1], recv_sem=cross_rsem.at[which, k, i - 1],
            device_id=(y * nx + other, me), device_id_type=MESH,
        )

    def x_copy(which, s, i):
        other = (xh + i) % nx
        return pltpu.make_async_remote_copy(
            src_ref=x_send.at[which, s, pl.ds(pl.multiple_of(other * piece, piece), piece)],
            dst_ref=x_recv.at[which, s, i - 1],
            send_sem=x_ssem.at[which, s, i - 1], recv_sem=x_rsem.at[which, s, i - 1],
            device_id=(y * nx + other, me), device_id_type=MESH,
        )

    def summed(k, which, s):
        total = own[which, k, :, s * SUB : (s + 1) * SUB]
        if k > 0:
            ring_copy(which, k - 1, s).wait_recv()
            total = total + ring_recv[which, k - 1, s].astype(F32)
        return total

    def hop(k, s):
        for which in range(2):
            total = summed(k, which, s)
            if k < last:
                ring_send[which, k, s] = total.astype(BF)
                ring_copy(which, k, s).start()
            else:
                chunk[which, s] = total
                x_send[which, s] = total.astype(BF)
                for i in range(1, nx):
                    x_copy(which, s, i).start()

    def hops(t, between=()):
        todo = [(t, s) for s in range(AHEAD)] if t <= last else []
        if t >= LAG:
            todo += [(t - LAG, s) for s in range(AHEAD, subs)]
        for n in range(max(len(todo), len(between))):
            if n < len(todo):
                hop(*todo[n])
            if n < len(between):
                between[n]()

    def terms(k):
        for which in range(2):
            part = arrived[k, :, which * half : (which + 1) * half]
            product = dot(part, scaled[...], 0)
            own[which, k] = product[:, :cross_at]
            cross_send[which, k] = product[:, cross_at:].astype(BF)

    def cross_step(k):
        for which in range(2):
            for i in range(1, nx):
                cross_copy(which, k, i).start()

    own_piece = pl.ds(pl.multiple_of(xh * piece, piece), piece)

    def column_step(k, final=False):
        for which in range(2):
            total = cross_send[which, k, own_piece, :].astype(F32)
            for i in range(1, nx):
                cross_copy(which, k, i).wait_recv()
                total = total + cross_recv[which, k, i - 1].astype(F32)
            if k > 0:
                column_copy(which, k - 1).wait_recv()
                total = total + column_recv[which, k].astype(F32)
            if final:
                grad_out[which * piece : (which + 1) * piece, cross_at:] = total
            else:
                column_send[which, k] = total.astype(BF)
                column_copy(which, k).start()

    def pull(k, w):
        at = chunk_at(w, k) * span + w * piece
        part = jnp.concatenate(
            [
                weight[pl.ds(pl.multiple_of(at + 2 * piece * q, piece), piece), :]
                for q in range(nx)
            ],
            axis=0,
        )
        pulled[...] += dot(arrived[k, :, w * half : (w + 1) * half], part)

    out = take_edge(0, 0)
    to_peers(lambda peer: row_copy(1, peer))
    for g in range(groups):
        scale[g * rows : (g + 1) * rows, :] = out[4 * rows :, g * lanes : (g + 1) * lanes]
    scaled[...] = (scale[:, :1] * hidden[...]).astype(BF)
    terms(0)
    hops(0)
    cross_step(0)
    pull(0, 0)
    pull(0, 1)
    for d in range(last // 2):
        take(d)
        if d < last // 2 - 2:
            to_peers(functools.partial(row_copy, d + 2))
        elif d == last // 2 - 2:
            to_peers(functools.partial(edge_copy, 1))
        for k in (2 * d + 1, 2 * d + 2):
            terms(k)
            hops(
                k,
                (
                    functools.partial(cross_step, k),
                    functools.partial(pull, k, 0),
                    functools.partial(column_step, k - 1),
                    functools.partial(pull, k, 1),
                ),
            )

    take_edge(1, last)
    terms(last)
    hops(
        last,
        (
            functools.partial(cross_step, last),
            functools.partial(pull, last, 0),
            functools.partial(pull, last, 1),
        ),
    )
    router = jnp.sum(pulled[...] * hidden[...], axis=1, keepdims=True)
    router_send[...] = dot(
        select[...], jnp.broadcast_to(router, (slots, lanes)), 0, precision=lax.Precision.HIGHEST
    )
    to_peers(router_copy)
    router_recv[mine8, :] = router_send[mine8, :]
    column_step(last - 1)
    hops(last + 1)
    g = saved[:, :width].astype(F32)
    u = saved[:, width:].astype(F32)
    sg = jax.nn.sigmoid(g)
    dh = scale[:, :1] * pulled[...]
    pair_out[:, :width] = (dh * u * sg * (1.0 + g * (1.0 - sg))).astype(BF)
    pair_out[:, width:] = (dh * g * sg).astype(BF)

    hops(last + 2)
    column_step(last, final=True)
    wait_all(router_recv, 8, router_rsem)
    token = dot(place8[...], router_recv[...], precision=lax.Precision.HIGHEST)
    token_out[...] = jnp.sum(jnp.where(eye, token, 0.0), axis=0, keepdims=True)

    for t in range(last + 3, last + LAG + 1):
        hops(t)

    wait_all(router_send, 8, router_ssem)
    for e in range(2):
        wait_all(edge_send.at[e], 32, edge_ssem.at[e])

    @pl.loop(0, last // 2)
    def _(d):
        wait_all(send.at[d], msg, send_sem.at[d])

    @pl.loop(0, last)
    def _(k):
        for which in range(2):
            column_copy(which, k).wait_send()
            for s in range(subs):
                ring_copy(which, k, s).wait_send()

    @pl.loop(0, ny)
    def _(k):
        for which in range(2):
            for i in range(1, nx):
                cross_copy(which, k, i).wait_send()

    for s in range(subs):
        for which in range(2):
            total = chunk[which, s, own_piece, :]
            for i in range(1, nx):
                x_copy(which, s, i).wait_recv()
                total = total + x_recv[which, s, i - 1].astype(F32)
            grad_out[which * piece : (which + 1) * piece, s * SUB : (s + 1) * SUB] = total
            for i in range(1, nx):
                x_copy(which, s, i).wait_send()


def hand_on(*refs):
    count = (len(refs) - 2) // 3
    source, target, held = refs[:count], refs[count : 2 * count], refs[2 * count : 3 * count]
    arrive, leave = refs[3 * count :]
    incoming = [pltpu.make_async_copy(source[i], held[i], arrive.at[i]) for i in range(count)]
    outgoing = [pltpu.make_async_copy(held[i], target[i], leave.at[i]) for i in range(count)]
    for copy in incoming:
        copy.start()
    for first, second in zip(incoming, outgoing):
        first.wait()
        second.start()
    for copy in outgoing:
        copy.wait()


def shards(nx, cotangent, routes, gate_weight, down_weight, saved_pre):
    peers = lax.axis_size("exp")
    ny = lax.axis_size("rep") // nx
    tokens, model = cotangent.shape
    slots, double = saved_pre.shape[2:]
    width = double // 2
    half = model // ny // 2
    last = ny - 1
    pairs = last // 2
    piece = half // nx
    msg = GROUP * CAP
    block = GROUP * msg
    vmem = pl.BlockSpec(memory_space=pltpu.VMEM)
    dma = pltpu.SemaphoreType.DMA
    subs = (width - CROSS) // SUB
    results = pl.pallas_call(
        functools.partial(kernel, ny, nx, peers),
        out_shape=(
            jax.ShapeDtypeStruct((2 * piece, width), F32),
            jax.ShapeDtypeStruct((slots, double), BF),
            jax.ShapeDtypeStruct((1, tokens), F32),
        ),
        in_specs=[vmem, vmem, vmem, pl.BlockSpec(memory_space=pl.ANY), vmem],
        out_specs=(vmem, vmem, vmem),
        scratch_shapes=[
            pltpu.VMEM((model, width), BF),
            pltpu.VMEM((pairs, peers * msg, 128), BF),
            pltpu.VMEM((pairs, peers * msg, 128), BF),
            pltpu.VMEM((2, peers * 32, 128), BF),
            pltpu.VMEM((2, peers * 32, 128), BF),
            pltpu.VMEM((ny, slots, 2 * half), BF),
            pltpu.VMEM((tokens, slots), BF),
            pltpu.VMEM((tokens, peers * 8), F32),
            pltpu.VMEM((block, block), BF),
            pltpu.VMEM((GROUP * 32, 5 * msg), BF),
            pltpu.VMEM((2, 2 * half, half), BF),
            pltpu.VMEM((slots, peers * 8), F32),
            pltpu.VMEM((peers * 8, 128), F32),
            pltpu.VMEM((peers * 8, 128), F32),
            pltpu.VMEM((slots, width), F32),
            pltpu.VMEM((slots, 128), F32),
            pltpu.VMEM((slots, width), BF),
            pltpu.VMEM((slots, width), F32),
            pltpu.VMEM((2, ny, half, width - CROSS), F32),
            pltpu.VMEM((2, last, subs, half, SUB), BF),
            pltpu.VMEM((2, last, subs, half, SUB), BF),
            pltpu.VMEM((2, subs, half, SUB), F32),
            pltpu.VMEM((2, subs, half, SUB), BF),
            pltpu.VMEM((2, subs, nx - 1, piece, SUB), BF),
            pltpu.VMEM((2, ny, half, CROSS), BF),
            pltpu.VMEM((2, ny, nx - 1, piece, CROSS), BF),
            pltpu.VMEM((2, last, piece, CROSS), BF),
            pltpu.VMEM((2, ny, piece, CROSS), BF),
            dma, dma((pairs,)), dma((pairs,)), dma((2,)), dma((2,)), dma, dma,
            dma((2, last, subs)), dma((2, last, subs)),
            dma((2, subs, nx - 1)), dma((2, subs, nx - 1)),
            dma((2, ny, nx - 1)), dma((2, ny, nx - 1)), dma((2, last)), dma((2, last)),
        ],
        compiler_params=pltpu.CompilerParams(
            collective_id=0, has_side_effects=True, vmem_limit_bytes=56 * 1024 * 1024
        ),
        cost_estimate=pl.CostEstimate(
            flops=4 * slots * model * width, bytes_accessed=12 * 1024 * 1024, transcendentals=0
        ),
        name="expert_backward",
    )(
        cotangent,
        routes.reshape(1, tokens),
        gate_weight.reshape(1, tokens),
        down_weight[0],
        saved_pre[0, 0],
    )
    place = pl.BlockSpec(memory_space=pl.ANY)
    grad, pair, token = pl.pallas_call(
        hand_on,
        out_shape=tuple(jax.ShapeDtypeStruct(r.shape, r.dtype) for r in results),
        in_specs=[place] * 3,
        out_specs=(place,) * 3,
        scratch_shapes=[pltpu.VMEM(r.shape, r.dtype) for r in results] + [dma((3,)), dma((3,))],
        name="results",
    )(*results)
    return grad[None], pair[None, None], token.reshape(tokens, 1)


def solution(mesh):
    nx = 4 if mesh.shape["rep"] == 32 else 2
    in_specs = (
        P(("rep", "exp"), None),
        P(("rep", "exp"), None),
        P(("rep", "exp"), None),
        P("exp", None, None),
        P("rep", "exp", None, None),
    )
    out_specs = (P("exp", "rep", None), P("rep", "exp", None, None), P(("rep", "exp"), None))
    return jax.shard_map(
        functools.partial(shards, nx), mesh=mesh, in_specs=in_specs, out_specs=out_specs,
        check_vma=False,
    )
```
